256 devices in a mesh: pipe: 8 (over y, core), feat: 32 (over x, z).
Axes of the slice: x: 4, y: 4, z: 8, core: 2. Of those that a mesh axis runs over, the one named last changes fastest.
Arguments:
- grad_out: bfloat16 [512, 8192], P(None, 'feat'), may hold values from -6 to 6
- saved_input: bfloat16 [8, 512, 8192], P('pipe', None, 'feat'), may hold values from -6 to 6
- saved_first: bfloat16 [8, 512, 8192], P('pipe', None, 'feat'), may hold values from -6 to 6
- saved_pre: bfloat16 [8, 512, 8192], P('pipe', None, 'feat'), may hold values from -6 to 6
- saved_second: bfloat16 [8, 512, 8192], P('pipe', None, 'feat'), may hold values from -6 to 6
- right_one: bfloat16 [8, 64, 128, 128], P('pipe', 'feat'), may hold values from -0.5 to 0.5
- left_one: bfloat16 [8, 64, 128, 128], P('pipe', 'feat'), may hold values from -0.5 to 0.5
- right_two: bfloat16 [8, 64, 128, 128], P('pipe', 'feat'), may hold values from -0.5 to 0.5
- left_two: bfloat16 [8, 64, 128, 128], P('pipe', 'feat'), may hold values from -0.5 to 0.5
Outputs:
- grad_input: bfloat16 [8, 512, 8192], P('pipe', None, 'feat')
- grad_right_one: bfloat16 [8, 64, 128, 128], P('pipe', 'feat')
- grad_left_one: bfloat16 [8, 64, 128, 128], P('pipe', 'feat')
- grad_right_two: bfloat16 [8, 64, 128, 128], P('pipe', 'feat')
- grad_left_two: bfloat16 [8, 64, 128, 128], P('pipe', 'feat')
The draws below stay inside these ranges and needn't reach their ends.
All inputs are finite; a program needn't handle non-finite values.
Results may differ from the reference program's by a relative error of at most 0.034.
Values may be sent and summed in bfloat16 or wider, within the bound.
No kernel may reach another device: no remote copies, remote signals or barrier semaphores. Data moves between devices by JAX's collectives and lax.ppermute only.
A program may use at most 64 MiB of HBM per device.

```python
import jax
import jax.numpy as jnp

NB = 64
BS = 128
H = 2
D = 8192
TOK = 512
SECTIONS = 8


def block_levels(key, extent, pieces, low, largest):
    loudness, own = 1.0, jax.random.fold_in(key, 6)
    for dim, blocks in pieces:
        heights = jnp.exp(jax.random.uniform(jax.random.fold_in(own, dim), (blocks,), jnp.float32, low / len(pieces), largest / len(pieces)))
        loudness = loudness * jnp.repeat(heights, extent[dim] // blocks).reshape([-1 if axis == dim else 1 for axis in range(len(extent))])
    return loudness


def centred(stream_key, dims, width, most, pieces=(), held_as=jnp.bfloat16):
    values = width * jax.random.normal(stream_key, dims, jnp.float32)
    if pieces:
        values = values * block_levels(stream_key, dims, pieces, -0.22, 0.18)
    return jnp.clip(values, -most, most).astype(held_as)


def setup_inputs(seed: int = 0) -> dict:
    key_list = jax.random.split(jax.random.key(seed), 10)
    return {
        "grad_out": centred(key_list[0], (TOK, D), 1.0, 6.0, ((1, 32),)),
        "saved_input": centred(key_list[1], (SECTIONS, TOK, D), 1.0, 6.0, ((0, 8), (2, 32))),
        "saved_first": centred(key_list[2], (SECTIONS, TOK, D), 1.0, 6.0, ((0, 8), (2, 32))),
        "saved_pre": centred(key_list[3], (SECTIONS, TOK, D), 1.0, 6.0, ((0, 8), (2, 32))),
        "saved_second": centred(key_list[4], (SECTIONS, TOK, D), 1.0, 6.0, ((0, 8), (2, 32))),
        "right_one": centred(key_list[5], (SECTIONS, NB, BS, BS), BS ** -0.5, 0.5, ((0, 8), (1, 32))),
        "left_one": centred(key_list[6], (SECTIONS, NB, BS, BS), BS ** -0.5, 0.5, ((0, 8), (1, 32))),
        "right_two": centred(key_list[7], (SECTIONS, NB, BS, BS), BS ** -0.5, 0.5, ((0, 8), (1, 32))),
        "left_two": centred(key_list[8], (SECTIONS, NB, BS, BS), BS ** -0.5, 0.5, ((0, 8), (1, 32))),
    }


def permute(v):
    t = v.shape[0]
    return v.reshape(t, NB, H, NB).transpose(0, 3, 2, 1).reshape(t, NB * BS)

def apply_transposed(v, weight):
    t = v.shape[0]
    out = jnp.einsum('tkj,kij->tki', v.reshape(t, NB, BS).astype(jnp.float32), weight.astype(jnp.float32))
    return out.reshape(t, NB * BS)

def weight_grad(left, right):
    t = left.shape[0]
    return jnp.einsum('tki,tkj->kij', left.reshape(t, NB, BS).astype(jnp.float32), right.reshape(t, NB, BS).astype(jnp.float32)).astype(jnp.bfloat16)

def normal_cdf(z):
    return 0.5 * (1.0 + jax.scipy.special.erf(z * 0.7071067811865476))

def reference(grad_out, saved_input, saved_first, saved_pre, saved_second, right_one, left_one, right_two, left_two):
    dy = grad_out
    grads_in, grads_r1, grads_l1, grads_r2, grads_l2 = ([], [], [], [], [])
    for section in range(SECTIONS - 1, -1, -1):
        out2 = permute(dy)
        grads_l2.append(weight_grad(saved_second[section], out2))
        back2 = apply_transposed(out2, left_two[section]).astype(jnp.bfloat16)
        mid2 = permute(back2)
        z = saved_pre[section].astype(jnp.float32)
        cdf = normal_cdf(z)
        act = (z * cdf).astype(jnp.bfloat16)
        grads_r2.append(weight_grad(act, mid2))
        slope = cdf + z * jnp.exp(-0.5 * z * z) * 0.3989422804014327
        pre_grad = (apply_transposed(mid2, right_two[section]) * slope).astype(jnp.bfloat16)
        out1 = permute(pre_grad)
        grads_l1.append(weight_grad(saved_first[section], out1))
        back1 = apply_transposed(out1, left_one[section]).astype(jnp.bfloat16)
        mid1 = permute(back1)
        grads_r1.append(weight_grad(saved_input[section], mid1))
        dy = (dy.astype(jnp.float32) + apply_transposed(mid1, right_one[section])).astype(jnp.bfloat16)
        grads_in.append(dy)
    order = lambda items: jnp.stack(items[::-1])
    return (order(grads_in), order(grads_r1), order(grads_l1), order(grads_r2), order(grads_l2))
```

```python
import functools

import jax
import jax.numpy as jnp
from jax import lax
from jax.experimental import pallas as pl
from jax.experimental.pallas import tpu as pltpu
from jax.sharding import PartitionSpec as P

BS = 128
BF = jnp.bfloat16
F32 = jnp.float32


def permuted(src, dst, tok):
    nb = src.shape[0] // tok
    low = lax.broadcasted_iota(jnp.int32, (nb, BS), 1) < nb
    for t in range(0, tok, 2):
        a = src[pl.ds(t, nb, stride=tok), :]
        b = src[pl.ds(t + 1, nb, stride=tok), :]
        y = jnp.concatenate([a, b], axis=0).T
        top, bot = y[:nb], y[nb:]
        dst[pl.ds(t, nb, stride=tok), :] = jnp.where(low, top, pltpu.roll(bot, nb, 1))
        dst[pl.ds(t + 1, nb, stride=tok), :] = jnp.where(low, pltpu.roll(top, nb, 1), bot)


def section_kernel(
    active, dy_hbm, slope_hbm, w_hbm, e_old, e_hbm, gx_hbm,
    dy, slope, w, e, s1, s2, in_sem, w_sem, out_sem,
):
    nsrc, tok, width = dy.shape

    def lanes(k):
        return pl.ds(k * BS, BS)

    def rows(blk):
        return pl.ds(blk * tok, tok)

    @pl.when(active[0] == 1)
    def _():
        get_dy = pltpu.make_async_copy(dy_hbm, dy, in_sem.at[0])
        get_slope = pltpu.make_async_copy(slope_hbm, slope, in_sem.at[1])
        get_w = [
            pltpu.make_async_copy(w_hbm.at[:, pl.ds(2 * f, 2)], w.at[:, pl.ds(2 * f, 2)], w_sem.at[f])
            for f in range(4)
        ]
        put_e = [
            pltpu.make_async_copy(
                e.at[:, pl.ds(f * tok, tok)], e_hbm.at[:, pl.ds(f * tok, tok)], out_sem.at[f]
            )
            for f in range(5)
        ]
        put_gx = pltpu.make_async_copy(e.at[:, pl.ds(4 * tok, tok)], gx_hbm, out_sem.at[5])
        get_dy.start()
        get_w[0].start()
        get_w[1].start()
        get_slope.start()
        get_w[2].start()
        get_w[3].start()
        get_dy.wait()
        for s in range(nsrc):
            for k in range(2):
                s1[rows(2 * s + k), :] = dy[s, :, k * BS:(k + 1) * BS].astype(F32)
        for f in range(4):
            permuted(s1, s2, tok)
            get_w[f].wait()
            if f == 1:
                get_slope.wait()
            for s in range(nsrc):
                for k in range(2):
                    v = s2[rows(2 * s + k), :].astype(BF)
                    e[s, f * tok:(f + 1) * tok, k * BS:(k + 1) * BS] = v
                    out = jnp.dot(v, w[s, 2 * f + k], preferred_element_type=F32)
                    if f == 1:
                        out = out * slope[s, :, k * BS:(k + 1) * BS]
                    if f < 3:
                        s1[rows(2 * s + k), :] = out.astype(BF).astype(F32)
                    else:
                        out = out + dy[s, :, k * BS:(k + 1) * BS].astype(F32)
                        e[s, 4 * tok:5 * tok, k * BS:(k + 1) * BS] = out.astype(BF)
            put_e[f].start()
        put_gx.start()
        put_e[4].start()
        put_gx.wait()
        for f in range(5):
            put_e[f].wait()


def section(active, dy, slope, w, e):
    nsrc, tok, width = dy.shape
    anywhere = pl.BlockSpec(memory_space=pl.ANY)
    return pl.pallas_call(
        section_kernel,
        out_shape=(
            jax.ShapeDtypeStruct(e.shape, BF),
            jax.ShapeDtypeStruct(dy.shape, BF),
        ),
        in_specs=[pl.BlockSpec(memory_space=pltpu.SMEM)] + [anywhere] * 4,
        out_specs=(anywhere, anywhere),
        input_output_aliases={4: 0},
        scratch_shapes=[
            pltpu.VMEM(dy.shape, BF),
            pltpu.VMEM(slope.shape, F32),
            pltpu.VMEM(w.shape, BF),
            pltpu.VMEM(e.shape, BF),
            pltpu.VMEM((nsrc * 2 * tok, BS), F32),
            pltpu.VMEM((nsrc * 2 * tok, BS), F32),
            pltpu.SemaphoreType.DMA((2,)),
            pltpu.SemaphoreType.DMA((4,)),
            pltpu.SemaphoreType.DMA((6,)),
        ],
        compiler_params=pltpu.CompilerParams(vmem_limit_bytes=32 * 1024 * 1024),
        name="section",
    )(active, dy, slope, w, e)


def grads_kernel(tok, e, l2, r2, l1, r1, gx, g_r1, g_l1, g_r2, g_l2):
    nsrc = e.shape[0]
    for f, (left, out) in enumerate(((l2, g_l2), (r2, g_r2), (l1, g_l1), (r1, g_r1))):
        right = e[:, f * tok:(f + 1) * tok, :].reshape(nsrc * tok, -1)
        for k in range(2):
            cols = slice(k * BS, (k + 1) * BS)
            out[0, k] = lax.dot_general(
                left[0, :, cols], right[:, cols], (((0,), (0,)), ((), ())),
                preferred_element_type=F32,
            ).astype(BF)
    gx[0] = e[:, 4 * tok:5 * tok, :].reshape(nsrc * tok, -1)


def weight_grads(tok, e, l2, r2, l1, r1, w_shape):
    vmem = pl.BlockSpec(memory_space=pltpu.VMEM)
    return pl.pallas_call(
        functools.partial(grads_kernel, tok),
        out_shape=(jax.ShapeDtypeStruct(l2.shape, BF),)
        + tuple(jax.ShapeDtypeStruct(w_shape, BF) for _ in range(4)),
        in_specs=[vmem] * 5,
        out_specs=(vmem,) * 5,
        compiler_params=pltpu.CompilerParams(vmem_limit_bytes=32 * 1024 * 1024),
        name="weight_grads",
    )(e, l2, r2, l1, r1)


def shards(
    grad_out, saved_input, saved_first, saved_pre, saved_second,
    right_one, left_one, right_two, left_two,
):
    me = lax.axis_index("pipe")
    nsec = lax.axis_size("pipe")
    nfeat = lax.axis_size("feat")
    ntok, width = grad_out.shape
    tok = ntok // nfeat

    own = jnp.concatenate([left_two[0], right_two[0], left_one[0], right_one[0]], axis=0)
    own = jnp.swapaxes(own, 1, 2)
    w = lax.all_gather(own, "feat", axis=0, tiled=True).reshape(nfeat, 8, BS, BS)

    both = jnp.concatenate(
        [saved_pre[0].reshape(nfeat, tok, width), grad_out.reshape(nfeat, tok, width)], axis=1
    )
    both = lax.all_to_all(both, "feat", split_axis=0, concat_axis=0, tiled=True)
    z = both[:, :tok].astype(F32)
    dy = both[:, tok:]
    cdf = 0.5 * (1.0 + lax.erf(z * 0.7071067811865476))
    slope = cdf + z * jnp.exp(-0.5 * z * z) * 0.3989422804014327
    zf = saved_pre.astype(F32)
    act = (zf * (0.5 * (1.0 + lax.erf(zf * 0.7071067811865476)))).astype(BF)

    e = jnp.zeros((nfeat, 5 * tok, width), BF)
    for turn in range(nsec):
        sec = nsec - 1 - turn
        active = (me == sec).astype(jnp.int32).reshape(1)
        e, gx = section(active, dy, slope, w, e)
        if sec > 0:
            dy = lax.ppermute(gx, "pipe", [(sec, sec - 1)])
    e = lax.all_to_all(e, "feat", split_axis=0, concat_axis=0, tiled=True)
    return weight_grads(tok, e, saved_second, act, saved_first, saved_input, right_one.shape)


def solution(mesh):
    rows = P("pipe", None, "feat")
    blocks = P("pipe", "feat", None, None)
    return jax.shard_map(
        shards,
        mesh=mesh,
        in_specs=(P(None, "feat"),) + (rows,) * 4 + (blocks,) * 4,
        out_specs=(rows,) + (blocks,) * 4,
        check_vma=False,
    )
```

```python
import functools

import jax
import jax.numpy as jnp
from jax import lax
from jax.experimental import pallas as pl
from jax.experimental.pallas import tpu as pltpu
from jax.sharding import PartitionSpec as P

BS = 128
BF = jnp.bfloat16
F32 = jnp.float32


def permuted(src, dst, tok):
    nb = src.shape[0] // tok
    low = lax.broadcasted_iota(jnp.int32, (nb, BS), 1) < nb
    for t in range(0, tok, 2):
        a = src[pl.ds(t, nb, stride=tok), :]
        b = src[pl.ds(t + 1, nb, stride=tok), :]
        y = jnp.concatenate([a, b], axis=0).T
        top, bot = y[:nb], y[nb:]
        dst[pl.ds(t, nb, stride=tok), :] = jnp.where(low, top, pltpu.roll(bot, nb, 1))
        dst[pl.ds(t + 1, nb, stride=tok), :] = jnp.where(low, pltpu.roll(top, nb, 1), bot)


def section_kernel(again, active, dy, slope, w, *rest):
    e, gx, s1, s2 = rest[1:] if again else rest
    nsrc, tok, width = dy.shape

    def rows(blk):
        return pl.ds(blk * tok, tok)

    @pl.when(active[0] == 1)
    def _():
        first = lax.broadcasted_iota(jnp.int32, (tok, width), 1) < BS
        zero = jnp.zeros((tok, width), BF)
        for s in range(nsrc):
            for k in range(2):
                s1[rows(2 * s + k), :] = dy[s, :, k * BS:(k + 1) * BS].astype(F32)
        for f in range(4):
            permuted(s1, s2, tok)
            for s in range(nsrc):
                v = jnp.concatenate([s2[rows(2 * s), :].astype(BF), s2[rows(2 * s + 1), :].astype(BF)], axis=1)
                e[s, f * tok:(f + 1) * tok, :] = v
                pair = jnp.concatenate([jnp.where(first, v, zero), jnp.where(first, zero, v)], axis=0)
                out = jnp.dot(pair, w[s, 2 * f:2 * f + 2].reshape(width, BS), preferred_element_type=F32)
                if f == 1:
                    out = out * jnp.concatenate([slope[s, :, :BS], slope[s, :, BS:]], axis=0)
                if f < 3:
                    s1[pl.ds(2 * s * tok, 2 * tok), :] = out.astype(BF).astype(F32)
                else:
                    out = jnp.concatenate([out[:tok], out[tok:]], axis=1)
                    out = (out + dy[s].astype(F32)).astype(BF)
                    e[s, 4 * tok:5 * tok, :] = out
                    gx[s] = out


def in_vmem(v):
    return pltpu.with_memory_space_constraint(v, pltpu.VMEM)


def section(active, dy, slope, w, e):
    nsrc, tok, width = dy.shape
    smem = pl.BlockSpec(memory_space=pltpu.SMEM)
    vmem = pl.BlockSpec(memory_space=pltpu.VMEM)
    held = [in_vmem(dy), in_vmem(slope), in_vmem(w)]
    if e is not None:
        held.append(in_vmem(e))
    return pl.pallas_call(
        functools.partial(section_kernel, e is not None),
        out_shape=(pltpu.VMEM((nsrc, 5 * tok, width), BF), pltpu.VMEM(dy.shape, BF)),
        in_specs=[smem] + [vmem] * len(held),
        out_specs=(vmem, vmem),
        input_output_aliases={} if e is None else {4: 0},
        scratch_shapes=[pltpu.VMEM((nsrc * 2 * tok, BS), F32)] * 2,
        compiler_params=pltpu.CompilerParams(vmem_limit_bytes=16 * 1024 * 1024),
        name="section",
    )(active, *held)


def pack_kernel(l2, r2, l1, r1, out):
    for f, w in enumerate((l2, r2, l1, r1)):
        for k in range(2):
            out[2 * f + k] = w[0, k].astype(F32).T.astype(BF)


def pack(l2, r2, l1, r1):
    vmem = pl.BlockSpec(memory_space=pltpu.VMEM)
    return pl.pallas_call(
        pack_kernel,
        out_shape=jax.ShapeDtypeStruct((8, BS, BS), BF),
        in_specs=[vmem] * 4,
        out_specs=vmem,
        name="pack",
    )(l2, r2, l1, r1)


def grads_kernel(tok, e, l2, r2, l1, r1, gx, g_r1, g_l1, g_r2, g_l2):
    nsrc = e.shape[0]
    for f, (left, out) in enumerate(((l2, g_l2), (r2, g_r2), (l1, g_l1), (r1, g_r1))):
        right = e[:, f * tok:(f + 1) * tok, :].reshape(nsrc * tok, -1)
        for k in range(2):
            cols = slice(k * BS, (k + 1) * BS)
            out[0, k] = lax.dot_general(
                left[0, :, cols], right[:, cols], (((0,), (0,)), ((), ())),
                preferred_element_type=F32,
            ).astype(BF)
    gx[0] = e[:, 4 * tok:5 * tok, :].reshape(nsrc * tok, -1)


def weight_grads(tok, e, l2, r2, l1, r1, w_shape):
    vmem = pl.BlockSpec(memory_space=pltpu.VMEM)
    return pl.pallas_call(
        functools.partial(grads_kernel, tok),
        out_shape=(jax.ShapeDtypeStruct(l2.shape, BF),)
        + tuple(jax.ShapeDtypeStruct(w_shape, BF) for _ in range(4)),
        in_specs=[vmem] * 5,
        out_specs=(vmem,) * 5,
        compiler_params=pltpu.CompilerParams(vmem_limit_bytes=32 * 1024 * 1024),
        name="weight_grads",
    )(e, l2, r2, l1, r1)


def shards(
    grad_out, saved_input, saved_first, saved_pre, saved_second,
    right_one, left_one, right_two, left_two,
):
    me = lax.axis_index("pipe")
    nsec = lax.axis_size("pipe")
    nfeat = lax.axis_size("feat")
    ntok, width = grad_out.shape
    tok = ntok // nfeat

    own = pack(left_two, right_two, left_one, right_one)
    w = lax.all_gather(own, "feat", axis=0, tiled=True).reshape(nfeat, 8, BS, BS)

    both = jnp.concatenate(
        [saved_pre[0].reshape(nfeat, tok, width), grad_out.reshape(nfeat, tok, width)], axis=1
    )
    both = lax.all_to_all(both, "feat", split_axis=0, concat_axis=0, tiled=True)
    z = both[:, :tok].astype(F32)
    dy = both[:, tok:]
    cdf = 0.5 * (1.0 + lax.erf(z * 0.7071067811865476))
    slope = cdf + z * jnp.exp(-0.5 * z * z) * 0.3989422804014327
    zf = saved_pre.astype(F32)
    act = (zf * (0.5 * (1.0 + lax.erf(zf * 0.7071067811865476)))).astype(BF)

    e = jnp.zeros((nfeat, 5 * tok, width), BF)
    for turn in range(nsec):
        sec = nsec - 1 - turn
        active = (me == sec).astype(jnp.int32).reshape(1)
        e, gx = section(active, dy, slope, w, e)
        if sec > 0:
            dy = lax.ppermute(gx, "pipe", [(sec, sec - 1)])
    e = lax.all_to_all(e, "feat", split_axis=0, concat_axis=0, tiled=True)
    return weight_grads(tok, e, saved_second, act, saved_first, saved_input, right_one.shape)


def solution(mesh):
    rows = P("pipe", None, "feat")
    blocks = P("pipe", "feat", None, None)
    return jax.shard_map(
        shards,
        mesh=mesh,
        in_specs=(P(None, "feat"),) + (rows,) * 4 + (blocks,) * 4,
        out_specs=(rows,) + (blocks,) * 4,
        check_vma=False,
    )
```

```python
import functools

import jax
import jax.numpy as jnp
from jax import lax
from jax.experimental import pallas as pl
from jax.experimental.pallas import tpu as pltpu
from jax.sharding import PartitionSpec as P

BS = 128
BF = jnp.bfloat16
F32 = jnp.float32


def permuted(src, dst, tok):
    nb = src.shape[0] // tok
    low = lax.broadcasted_iota(jnp.int32, (nb, BS), 1) < nb
    for t in range(0, tok, 2):
        a = src[pl.ds(t, nb, stride=tok), :]
        b = src[pl.ds(t + 1, nb, stride=tok), :]
        y = jnp.concatenate([a, b], axis=0).T
        top, bot = y[:nb], y[nb:]
        dst[pl.ds(t, nb, stride=tok), :] = jnp.where(low, top, pltpu.roll(bot, nb, 1))
        dst[pl.ds(t + 1, nb, stride=tok), :] = jnp.where(low, pltpu.roll(top, nb, 1), bot)


def section_kernel(last, active, dy, slope, w_hbm, e_old, *rest):
    if last:
        e_hbm, w, s1, s2, w_sems, e, sems = rest
    else:
        e, gx, w, s1, s2, w_sems = rest
    nsrc, tok, width = dy.shape

    def rows(blk):
        return pl.ds(blk * tok, tok)

    @pl.when(active[0] == 1)
    def _():
        gets = [
            pltpu.make_async_copy(w_hbm.at[:, pl.ds(2 * f, 2)], w.at[:, pl.ds(2 * f, 2)], w_sems.at[f])
            for f in range(4)
        ]
        for get in gets:
            get.start()
        if last:
            puts = [
                pltpu.make_async_copy(
                    e.at[:, pl.ds(f * tok, tok)], e_hbm.at[:, pl.ds(f * tok, tok)], sems.at[f]
                )
                for f in range(5)
            ]
        first = lax.broadcasted_iota(jnp.int32, (tok, width), 1) < BS
        zero = jnp.zeros((tok, width), BF)
        for s in range(nsrc):
            for k in range(2):
                s1[rows(2 * s + k), :] = dy[s, :, k * BS:(k + 1) * BS].astype(F32)
        for f in range(4):
            permuted(s1, s2, tok)
            gets[f].wait()
            for s in range(nsrc):
                v = jnp.concatenate([s2[rows(2 * s), :].astype(BF), s2[rows(2 * s + 1), :].astype(BF)], axis=1)
                e[s, f * tok:(f + 1) * tok, :] = v
                pair = jnp.concatenate([jnp.where(first, v, zero), jnp.where(first, zero, v)], axis=0)
                out = jnp.dot(pair, w[s, 2 * f:2 * f + 2].reshape(width, BS), preferred_element_type=F32)
                if f == 1:
                    out = out * jnp.concatenate([slope[s, :, :BS], slope[s, :, BS:]], axis=0)
                if f < 3:
                    s1[pl.ds(2 * s * tok, 2 * tok), :] = out.astype(BF).astype(F32)
                else:
                    out = jnp.concatenate([out[:tok], out[tok:]], axis=1)
                    out = (out + dy[s].astype(F32)).astype(BF)
                    e[s, 4 * tok:5 * tok, :] = out
                    if not last:
                        gx[s] = out
            if last:
                puts[f].start()
        if last:
            puts[4].start()
            for put in puts:
                put.wait()

    if last:
        @pl.when(active[0] == 0)
        def _():
            put = pltpu.make_async_copy(e_old, e_hbm, sems.at[0])
            put.start()
            put.wait()


def in_vmem(v):
    return pltpu.with_memory_space_constraint(v, pltpu.VMEM)


def section(active, dy, slope, w, e, last=False):
    nsrc, tok, width = dy.shape
    smem = pl.BlockSpec(memory_space=pltpu.SMEM)
    vmem = pl.BlockSpec(memory_space=pltpu.VMEM)
    anywhere = pl.BlockSpec(memory_space=pl.ANY)
    work = [
        pltpu.VMEM(w.shape, BF),
        pltpu.VMEM((nsrc * 2 * tok, BS), F32),
        pltpu.VMEM((nsrc * 2 * tok, BS), F32),
        pltpu.SemaphoreType.DMA((4,)),
    ]
    if last:
        out_shape = jax.ShapeDtypeStruct(e.shape, BF)
        out_specs, aliases = anywhere, {}
        work += [pltpu.VMEM(e.shape, BF), pltpu.SemaphoreType.DMA((5,))]
    else:
        out_shape = (pltpu.VMEM(e.shape, BF), pltpu.VMEM(dy.shape, BF))
        out_specs, aliases = (vmem, vmem), {4: 0}
    return pl.pallas_call(
        functools.partial(section_kernel, last),
        out_shape=out_shape,
        in_specs=[smem, vmem, vmem, anywhere, vmem],
        out_specs=out_specs,
        input_output_aliases=aliases,
        scratch_shapes=work,
        compiler_params=pltpu.CompilerParams(vmem_limit_bytes=20 * 1024 * 1024),
        name="section",
    )(active, in_vmem(dy), in_vmem(slope), pltpu.with_memory_space_constraint(w, pltpu.HBM), in_vmem(e))


def blank_kernel(e):
    e[0] = jnp.zeros(e.shape[1:], BF)


def blank(shape):
    return pl.pallas_call(
        blank_kernel,
        out_shape=pltpu.VMEM(shape, BF),
        out_specs=pl.BlockSpec(memory_space=pltpu.VMEM),
        name="blank",
    )()


def pack_kernel(l2, r2, l1, r1, out):
    for f, w in enumerate((l2, r2, l1, r1)):
        for k in range(2):
            out[2 * f + k] = w[0, k].astype(F32).T.astype(BF)


def pack(l2, r2, l1, r1):
    vmem = pl.BlockSpec(memory_space=pltpu.VMEM)
    return pl.pallas_call(
        pack_kernel,
        out_shape=jax.ShapeDtypeStruct((8, BS, BS), BF),
        in_specs=[vmem] * 4,
        out_specs=vmem,
        name="pack",
    )(l2, r2, l1, r1)


def grads_kernel(tok, e, l2, r2, l1, r1, gx, g_r1, g_l1, g_r2, g_l2):
    nsrc = e.shape[0]
    for f, (left, out) in enumerate(((l2, g_l2), (r2, g_r2), (l1, g_l1), (r1, g_r1))):
        right = e[:, f * tok:(f + 1) * tok, :].reshape(nsrc * tok, -1)
        for k in range(2):
            cols = slice(k * BS, (k + 1) * BS)
            out[0, k] = lax.dot_general(
                left[0, :, cols], right[:, cols], (((0,), (0,)), ((), ())),
                preferred_element_type=F32,
            ).astype(BF)
    gx[0] = e[:, 4 * tok:5 * tok, :].reshape(nsrc * tok, -1)


def weight_grads(tok, e, l2, r2, l1, r1, w_shape):
    vmem = pl.BlockSpec(memory_space=pltpu.VMEM)
    return pl.pallas_call(
        functools.partial(grads_kernel, tok),
        out_shape=(jax.ShapeDtypeStruct(l2.shape, BF),)
        + tuple(jax.ShapeDtypeStruct(w_shape, BF) for _ in range(4)),
        in_specs=[vmem] * 5,
        out_specs=(vmem,) * 5,
        compiler_params=pltpu.CompilerParams(vmem_limit_bytes=32 * 1024 * 1024),
        name="weight_grads",
    )(e, l2, r2, l1, r1)


def shards(
    grad_out, saved_input, saved_first, saved_pre, saved_second,
    right_one, left_one, right_two, left_two,
):
    me = lax.axis_index("pipe")
    nsec = lax.axis_size("pipe")
    nfeat = lax.axis_size("feat")
    ntok, width = grad_out.shape
    tok = ntok // nfeat

    own = pack(left_two, right_two, left_one, right_one)
    w = lax.all_gather(own, "feat", axis=0, tiled=True).reshape(nfeat, 8, BS, BS)

    both = jnp.concatenate(
        [saved_pre[0].reshape(nfeat, tok, width), grad_out.reshape(nfeat, tok, width)], axis=1
    )
    both = lax.all_to_all(both, "feat", split_axis=0, concat_axis=0, tiled=True)
    z = both[:, :tok].astype(F32)
    dy = both[:, tok:]
    cdf = 0.5 * (1.0 + lax.erf(z * 0.7071067811865476))
    slope = cdf + z * jnp.exp(-0.5 * z * z) * 0.3989422804014327
    zf = saved_pre.astype(F32)
    act = (zf * (0.5 * (1.0 + lax.erf(zf * 0.7071067811865476)))).astype(BF)

    e = blank((nfeat, 5 * tok, width))
    for turn in range(nsec):
        sec = nsec - 1 - turn
        active = (me == sec).astype(jnp.int32).reshape(1)
        if sec > 0:
            e, gx = section(active, dy, slope, w, e)
            dy = lax.ppermute(gx, "pipe", [(sec, sec - 1)])
        else:
            e = section(active, dy, slope, w, e, last=True)
    e = lax.all_to_all(e, "feat", split_axis=0, concat_axis=0, tiled=True)
    return weight_grads(tok, e, saved_second, act, saved_first, saved_input, right_one.shape)


def solution(mesh):
    rows = P("pipe", None, "feat")
    blocks = P("pipe", "feat", None, None)
    return jax.shard_map(
        shards,
        mesh=mesh,
        in_specs=(P(None, "feat"),) + (rows,) * 4 + (blocks,) * 4,
        out_specs=(rows,) + (blocks,) * 4,
        check_vma=False,
    )
```

```python
import functools

import jax
import jax.numpy as jnp
from jax import lax
from jax.experimental import pallas as pl
from jax.experimental.pallas import tpu as pltpu
from jax.sharding import PartitionSpec as P

BS = 128
BF = jnp.bfloat16
F32 = jnp.float32
NX, NZ = 4, 8
X_SLOTS = ((0, 0), (1, 0), (3, 0), (2, 0), (2, 1))
Z_SLOTS = ((0, 0), (1, 0), (7, 0), (2, 0), (6, 0), (3, 0), (5, 0), (4, 0), (4, 1))


def permuted(src, dst, tok):
    nb = src.shape[0] // tok
    low = lax.broadcasted_iota(jnp.int32, (nb, BS), 1) < nb
    for t in range(0, tok, 2):
        a = src[pl.ds(t, nb, stride=tok), :]
        b = src[pl.ds(t + 1, nb, stride=tok), :]
        y = jnp.concatenate([a, b], axis=0).T
        top, bot = y[:nb], y[nb:]
        dst[pl.ds(t, nb, stride=tok), :] = jnp.where(low, top, pltpu.roll(bot, nb, 1))
        dst[pl.ds(t + 1, nb, stride=tok), :] = jnp.where(low, pltpu.roll(top, nb, 1), bot)


def section_kernel(last, npieces, where, dy, slope, e_old, *rest):
    pieces, rest = rest[:npieces], rest[npieces:]
    if last:
        e_hbm, wa, wb, s1, s2, w_sems, e, sems = rest
    else:
        e, gx, wa, wb, s1, s2, w_sems = rest
    nsrc, tok, width = dy.shape

    def rows(blk):
        return pl.ds(blk * tok, tok)

    @pl.when(where[0] == 1)
    def _():
        gets = []
        for held, slots, parts, f, nblk in (
            (wa, X_SLOTS, pieces[:len(X_SLOTS)], 0, 2),
            (wa, X_SLOTS, pieces[:len(X_SLOTS)], 1, 2),
            (wb, Z_SLOTS, pieces[len(X_SLOTS):], 0, 4),
        ):
            blocks = pl.ds(2 * f, nblk)
            base = sum(map(len, gets))
            gets.append([
                pltpu.make_async_copy(
                    part.at[:, blocks],
                    held.at[slot, pl.ds(half * part.shape[0], part.shape[0]), blocks],
                    w_sems.at[base + i],
                )
                for i, (part, (slot, half)) in enumerate(zip(parts, slots))
            ])
        for group in gets:
            for get in group:
                get.start()
        if last:
            puts = [
                pltpu.make_async_copy(
                    e.at[:, pl.ds(f * tok, tok)], e_hbm.at[:, pl.ds(f * tok, tok)], sems.at[f]
                )
                for f in range(5)
            ]
        first = lax.broadcasted_iota(jnp.int32, (tok, width), 1) < BS
        zero = jnp.zeros((tok, width), BF)
        for s in range(nsrc):
            for k in range(2):
                s1[rows(2 * s + k), :] = dy[s, :, k * BS:(k + 1) * BS].astype(F32)
        for f in range(4):
            permuted(s1, s2, tok)
            for get in gets[f] if f < 3 else []:
                get.wait()
            for s in range(nsrc):
                v = jnp.concatenate([s2[rows(2 * s), :].astype(BF), s2[rows(2 * s + 1), :].astype(BF)], axis=1)
                e[s, f * tok:(f + 1) * tok, :] = v
                pair = jnp.concatenate([jnp.where(first, v, zero), jnp.where(first, zero, v)], axis=0)
                rx, rz = where[1 + s // NZ], where[1 + NX + s % NZ]
                if f < 2:
                    mat = wa[rx, rz, 2 * f:2 * f + 2]
                else:
                    mat = wb[rz, s // NZ, 2 * f - 4:2 * f - 2]
                out = jnp.dot(pair, mat.reshape(width, BS), preferred_element_type=F32)
                if f == 1:
                    out = out * jnp.concatenate([slope[s, :, :BS], slope[s, :, BS:]], axis=0)
                if f < 3:
                    s1[pl.ds(2 * s * tok, 2 * tok), :] = out.astype(BF).astype(F32)
                else:
                    out = jnp.concatenate([out[:tok], out[tok:]], axis=1)
                    out = (out + dy[s].astype(F32)).astype(BF)
                    e[s, 4 * tok:5 * tok, :] = out
                    if not last:
                        gx[s] = out
            if last:
                puts[f].start()
        if last:
            puts[4].start()
            for put in puts:
                put.wait()

    if last:
        @pl.when(where[0] == 0)
        def _():
            put = pltpu.make_async_copy(e_old, e_hbm, sems.at[0])
            put.start()
            put.wait()


def in_vmem(v):
    return pltpu.with_memory_space_constraint(v, pltpu.VMEM)


def section(where, dy, slope, pieces, e, last=False):
    nsrc, tok, width = dy.shape
    smem = pl.BlockSpec(memory_space=pltpu.SMEM)
    vmem = pl.BlockSpec(memory_space=pltpu.VMEM)
    anywhere = pl.BlockSpec(memory_space=pl.ANY)
    work = [
        pltpu.VMEM((NX, NZ, 4, BS, BS), BF),
        pltpu.VMEM((NZ, NX, 4, BS, BS), BF),
        pltpu.VMEM((nsrc * 2 * tok, BS), F32),
        pltpu.VMEM((nsrc * 2 * tok, BS), F32),
        pltpu.SemaphoreType.DMA((2 * len(pieces),)),
    ]
    if last:
        out_shape = jax.ShapeDtypeStruct(e.shape, BF)
        out_specs, aliases = anywhere, {}
        work += [pltpu.VMEM(e.shape, BF), pltpu.SemaphoreType.DMA((5,))]
    else:
        out_shape = (pltpu.VMEM(e.shape, BF), pltpu.VMEM(dy.shape, BF))
        out_specs, aliases = (vmem, vmem), {3: 0}
    return pl.pallas_call(
        functools.partial(section_kernel, last, len(pieces)),
        out_shape=out_shape,
        in_specs=[smem, vmem, vmem, vmem] + [anywhere] * len(pieces),
        out_specs=out_specs,
        input_output_aliases=aliases,
        scratch_shapes=work,
        compiler_params=pltpu.CompilerParams(vmem_limit_bytes=20 * 1024 * 1024),
        name="section",
    )(
        where, in_vmem(dy), in_vmem(slope), in_vmem(e),
        *[pltpu.with_memory_space_constraint(p, pltpu.HBM) for p in pieces],
    )


def shift(v, dx, dz):
    route = [
        (x * NZ + z, (x + dx) % NX * NZ + (z + dz) % NZ) for x in range(NX) for z in range(NZ)
    ]
    return lax.ppermute(v, "feat", route)


def along_z(v):
    half = v.shape[0] // 2
    up, down = shift(v, 0, -1), shift(v, 0, 1)
    out = [v, up, down]
    for _ in range(2):
        up, down = shift(up, 0, -1), shift(down, 0, 1)
        out += [up, down]
    return out + [shift(up[:half], 0, -1), shift(down[half:], 0, 1)]


def gathered(two, one, both):
    columns = [[x * NZ + z for x in range(NX)] for z in range(NZ)]
    one = lax.all_gather(one, "feat", axis=0, axis_index_groups=columns)
    both = lax.all_to_all(both, "feat", split_axis=0, concat_axis=0, tiled=True)
    own, u1, d1, u2, d2, u3, d3, u4, d4 = along_z(two)
    one, _ = lax.optimization_barrier((one, u2))
    two = jnp.stack([own, u1, u2, u3, jnp.concatenate([u4, d4]), d3, d2, d1])
    up, down = shift(one, 0, -1), shift(one, 0, 1)
    by_z = [one, up, down]
    x_up, x_down = shift(two, -1, 0), shift(two, 1, 0)
    up, down = shift(up, 0, -1), shift(down, 0, 1)
    by_z += [up, down]
    up, down = shift(up, 0, -1), shift(down, 0, 1)
    by_z += [up, down]
    half = NX // 2
    by_z += [shift(up[:half], 0, -1), shift(down[half:], 0, 1)]
    half = NZ // 2
    by_x = [two, x_up, x_down, shift(x_up[:half], -1, 0), shift(x_down[half:], 1, 0)]
    return by_x + by_z, both


def blank_kernel(e):
    e[0] = jnp.zeros(e.shape[1:], BF)


def blank(shape):
    return pl.pallas_call(
        blank_kernel,
        out_shape=pltpu.VMEM(shape, BF),
        out_specs=pl.BlockSpec(memory_space=pltpu.VMEM),
        name="blank",
    )()


def pack_kernel(l2, r2, l1, r1, two, one):
    for f, w in enumerate((l2, r2, l1, r1)):
        for k in range(2):
            (two, one)[f // 2][2 * (f % 2) + k] = w[0, k].astype(F32).T.astype(BF)


def pack(l2, r2, l1, r1):
    vmem = pl.BlockSpec(memory_space=pltpu.VMEM)
    return pl.pallas_call(
        pack_kernel,
        out_shape=(jax.ShapeDtypeStruct((4, BS, BS), BF),) * 2,
        in_specs=[vmem] * 4,
        out_specs=(vmem, vmem),
        name="pack",
    )(l2, r2, l1, r1)


def grads_kernel(tok, e, l2, r2, l1, r1, gx, g_r1, g_l1, g_r2, g_l2):
    nsrc = e.shape[0]
    for f, (left, out) in enumerate(((l2, g_l2), (r2, g_r2), (l1, g_l1), (r1, g_r1))):
        right = e[:, f * tok:(f + 1) * tok, :].reshape(nsrc * tok, -1)
        for k in range(2):
            cols = slice(k * BS, (k + 1) * BS)
            out[0, k] = lax.dot_general(
                left[0, :, cols], right[:, cols], (((0,), (0,)), ((), ())),
                preferred_element_type=F32,
            ).astype(BF)
    gx[0] = e[:, 4 * tok:5 * tok, :].reshape(nsrc * tok, -1)


def weight_grads(tok, e, l2, r2, l1, r1, w_shape):
    vmem = pl.BlockSpec(memory_space=pltpu.VMEM)
    return pl.pallas_call(
        functools.partial(grads_kernel, tok),
        out_shape=(jax.ShapeDtypeStruct(l2.shape, BF),)
        + tuple(jax.ShapeDtypeStruct(w_shape, BF) for _ in range(4)),
        in_specs=[vmem] * 5,
        out_specs=(vmem,) * 5,
        compiler_params=pltpu.CompilerParams(vmem_limit_bytes=32 * 1024 * 1024),
        name="weight_grads",
    )(e, l2, r2, l1, r1)


def shards(
    grad_out, saved_input, saved_first, saved_pre, saved_second,
    right_one, left_one, right_two, left_two,
):
    me = lax.axis_index("pipe")
    nsec = lax.axis_size("pipe")
    nfeat = lax.axis_size("feat")
    ntok, width = grad_out.shape
    tok = ntok // nfeat

    at = lax.axis_index("feat")
    offsets = jnp.concatenate([(jnp.arange(NX) - at // NZ) % NX, (jnp.arange(NZ) - at % NZ) % NZ])

    both = jnp.concatenate(
        [saved_pre[0].reshape(nfeat, tok, width), grad_out.reshape(nfeat, tok, width)], axis=1
    )
    pieces, both = gathered(*pack(left_two, right_two, left_one, right_one), both)
    z = both[:, :tok].astype(F32)
    dy = both[:, tok:]
    cdf = 0.5 * (1.0 + lax.erf(z * 0.7071067811865476))
    slope = cdf + z * jnp.exp(-0.5 * z * z) * 0.3989422804014327
    zf = saved_pre.astype(F32)
    act = (zf * (0.5 * (1.0 + lax.erf(zf * 0.7071067811865476)))).astype(BF)

    e = blank((nfeat, 5 * tok, width))
    for turn in range(nsec):
        sec = nsec - 1 - turn
        where = jnp.concatenate([(me == sec).astype(jnp.int32).reshape(1), offsets.astype(jnp.int32)])
        if sec > 0:
            e, gx = section(where, dy, slope, pieces, e)
            dy = lax.ppermute(gx, "pipe", [(sec, sec - 1)])
        else:
            e = section(where, dy, slope, pieces, e, last=True)
    e = lax.all_to_all(e, "feat", split_axis=0, concat_axis=0, tiled=True)
    return weight_grads(tok, e, saved_second, act, saved_first, saved_input, right_one.shape)


def solution(mesh):
    rows = P("pipe", None, "feat")
    blocks = P("pipe", "feat", None, None)
    return jax.shard_map(
        shards,
        mesh=mesh,
        in_specs=(P(None, "feat"),) + (rows,) * 4 + (blocks,) * 4,
        out_specs=(rows,) + (blocks,) * 4,
        check_vma=False,
    )
```

```python
import functools

import jax
import jax.numpy as jnp
from jax import lax
from jax.experimental import pallas as pl
from jax.experimental.pallas import tpu as pltpu
from jax.sharding import PartitionSpec as P

BS = 128
BF = jnp.bfloat16
F32 = jnp.float32
NX, NZ = 4, 8
X_SLOTS = ((0, 0), (1, 0), (3, 0), (2, 0), (2, 1))
Z_SLOTS = ((0, 0), (1, 0), (7, 0), (2, 0), (6, 0), (3, 0), (5, 0), (4, 0))


def permuted(src, dst, tok):
    nb = src.shape[0] // tok
    low = lax.broadcasted_iota(jnp.int32, (nb, BS), 1) < nb
    for t in range(0, tok, 2):
        a = src[pl.ds(t, nb, stride=tok), :]
        b = src[pl.ds(t + 1, nb, stride=tok), :]
        y = jnp.concatenate([a, b], axis=0).T
        top, bot = y[:nb], y[nb:]
        dst[pl.ds(t, nb, stride=tok), :] = jnp.where(low, top, pltpu.roll(bot, nb, 1))
        dst[pl.ds(t + 1, nb, stride=tok), :] = jnp.where(low, pltpu.roll(top, nb, 1), bot)


def section_kernel(last, npieces, where, dy, slope, e_old, *rest):
    pieces, rest = rest[:npieces], rest[npieces:]
    if last:
        e_hbm, wa, wb, s1, s2, w_sems, e, sems = rest
    else:
        e, gx, wa, wb, s1, s2, w_sems = rest
    nsrc, tok, width = dy.shape

    def rows(blk):
        return pl.ds(blk * tok, tok)

    @pl.when(where[0] == 1)
    def _():
        gets = []
        for held, slots, parts, f, nblk in (
            (wa, X_SLOTS, pieces[:len(X_SLOTS)], 0, 2),
            (wa, X_SLOTS, pieces[:len(X_SLOTS)], 1, 2),
            (wb, Z_SLOTS, pieces[len(X_SLOTS):], 0, 4),
        ):
            blocks = pl.ds(2 * f, nblk)
            base = sum(map(len, gets))
            gets.append([
                pltpu.make_async_copy(
                    part.at[:, blocks],
                    held.at[slot, pl.ds(half * part.shape[0], part.shape[0]), blocks],
                    w_sems.at[base + i],
                )
                for i, (part, (slot, half)) in enumerate(zip(parts, slots))
            ])
        for group in gets:
            for get in group:
                get.start()
        if last:
            puts = [
                pltpu.make_async_copy(
                    e.at[:, pl.ds(f * tok, tok)], e_hbm.at[:, pl.ds(f * tok, tok)], sems.at[f]
                )
                for f in range(5)
            ]
        first = lax.broadcasted_iota(jnp.int32, (tok, width), 1) < BS
        zero = jnp.zeros((tok, width), BF)
        for s in range(nsrc):
            for k in range(2):
                s1[rows(2 * s + k), :] = dy[s, :, k * BS:(k + 1) * BS].astype(F32)
        for f in range(4):
            permuted(s1, s2, tok)
            for get in gets[f] if f < 3 else []:
                get.wait()
            for s in range(nsrc):
                v = jnp.concatenate([s2[rows(2 * s), :].astype(BF), s2[rows(2 * s + 1), :].astype(BF)], axis=1)
                e[s, f * tok:(f + 1) * tok, :] = v
                pair = jnp.concatenate([jnp.where(first, v, zero), jnp.where(first, zero, v)], axis=0)
                rx, rz = where[1 + s // NZ], where[1 + NX + s % NZ]
                if f < 2:
                    mat = wa[rx, rz, 2 * f:2 * f + 2]
                else:
                    mat = wb[rz, rx, 2 * f - 4:2 * f - 2]
                out = jnp.dot(pair, mat.reshape(width, BS), preferred_element_type=F32)
                if f == 1:
                    out = out * jnp.concatenate([slope[s, :, :BS], slope[s, :, BS:]], axis=0)
                if f < 3:
                    s1[pl.ds(2 * s * tok, 2 * tok), :] = out.astype(BF).astype(F32)
                else:
                    out = jnp.concatenate([out[:tok], out[tok:]], axis=1)
                    out = (out + dy[s].astype(F32)).astype(BF)
                    e[s, 4 * tok:5 * tok, :] = out
                    if not last:
                        gx[s] = out
            if last:
                puts[f].start()
        if last:
            puts[4].start()
            for put in puts:
                put.wait()

    if last:
        @pl.when(where[0] == 0)
        def _():
            put = pltpu.make_async_copy(e_old, e_hbm, sems.at[0])
            put.start()
            put.wait()


def in_vmem(v):
    return pltpu.with_memory_space_constraint(v, pltpu.VMEM)


def section(where, dy, slope, pieces, e, last=False):
    nsrc, tok, width = dy.shape
    smem = pl.BlockSpec(memory_space=pltpu.SMEM)
    vmem = pl.BlockSpec(memory_space=pltpu.VMEM)
    anywhere = pl.BlockSpec(memory_space=pl.ANY)
    work = [
        pltpu.VMEM((NX, NZ, 4, BS, BS), BF),
        pltpu.VMEM((NZ, NX, 4, BS, BS), BF),
        pltpu.VMEM((nsrc * 2 * tok, BS), F32),
        pltpu.VMEM((nsrc * 2 * tok, BS), F32),
        pltpu.SemaphoreType.DMA((2 * len(pieces),)),
    ]
    if last:
        out_shape = jax.ShapeDtypeStruct(e.shape, BF)
        out_specs, aliases = anywhere, {}
        work += [pltpu.VMEM(e.shape, BF), pltpu.SemaphoreType.DMA((5,))]
    else:
        out_shape = (pltpu.VMEM(e.shape, BF), pltpu.VMEM(dy.shape, BF))
        out_specs, aliases = (vmem, vmem), {3: 0}
    return pl.pallas_call(
        functools.partial(section_kernel, last, len(pieces)),
        out_shape=out_shape,
        in_specs=[smem, vmem, vmem, vmem] + [anywhere] * len(pieces),
        out_specs=out_specs,
        input_output_aliases=aliases,
        scratch_shapes=work,
        compiler_params=pltpu.CompilerParams(vmem_limit_bytes=20 * 1024 * 1024),
        name="section",
    )(
        where, in_vmem(dy), in_vmem(slope), in_vmem(e),
        *[pltpu.with_memory_space_constraint(p, pltpu.HBM) for p in pieces],
    )


def shift(v, dx, dz):
    route = [
        (x * NZ + z, (x + dx) % NX * NZ + (z + dz) % NZ) for x in range(NX) for z in range(NZ)
    ]
    return lax.ppermute(v, "feat", route)


def along_z(v):
    up, down = shift(v, 0, -1), shift(v, 0, 1)
    out = [v, up, down]
    for _ in range(2):
        up, down = shift(up, 0, -1), shift(down, 0, 1)
        out += [up, down]
    return out + [shift(up, 0, -1)]


def gathered(two, one, both):
    one = jnp.stack([one, shift(one, -1, 0), shift(one, 2, 0), shift(one, 1, 0)])
    both = lax.all_to_all(both, "feat", split_axis=0, concat_axis=0, tiled=True)
    own, u1, d1, u2, d2, u3, d3, u4 = along_z(two)
    one, _ = lax.optimization_barrier((one, u2))
    two = jnp.stack([own, u1, u2, u3, u4, d3, d2, d1])
    up, down = shift(one, 0, -1), shift(one, 0, 1)
    by_z = [one, up, down]
    x_up, x_down = shift(two, -1, 0), shift(two, 1, 0)
    up, down = shift(up, 0, -1), shift(down, 0, 1)
    by_z += [up, down]
    up, down = shift(up, 0, -1), shift(down, 0, 1)
    by_z += [up, down]
    by_z += [shift(up, 0, -1)]
    half = NZ // 2
    by_x = [two, x_up, x_down, shift(x_up[:half], -1, 0), shift(x_down[half:], 1, 0)]
    return by_x + by_z, both


def blank_kernel(e):
    e[0] = jnp.zeros(e.shape[1:], BF)


def blank(shape):
    return pl.pallas_call(
        blank_kernel,
        out_shape=pltpu.VMEM(shape, BF),
        out_specs=pl.BlockSpec(memory_space=pltpu.VMEM),
        name="blank",
    )()


def pack_kernel(l2, r2, l1, r1, two, one):
    for f, w in enumerate((l2, r2, l1, r1)):
        for k in range(2):
            (two, one)[f // 2][2 * (f % 2) + k] = w[0, k].astype(F32).T.astype(BF)


def pack(l2, r2, l1, r1):
    vmem = pl.BlockSpec(memory_space=pltpu.VMEM)
    return pl.pallas_call(
        pack_kernel,
        out_shape=(jax.ShapeDtypeStruct((4, BS, BS), BF),) * 2,
        in_specs=[vmem] * 4,
        out_specs=(vmem, vmem),
        name="pack",
    )(l2, r2, l1, r1)


def grads_kernel(tok, e, l2, r2, l1, r1, gx, g_r1, g_l1, g_r2, g_l2):
    nsrc = e.shape[0]
    for f, (left, out) in enumerate(((l2, g_l2), (r2, g_r2), (l1, g_l1), (r1, g_r1))):
        right = e[:, f * tok:(f + 1) * tok, :].reshape(nsrc * tok, -1)
        for k in range(2):
            cols = slice(k * BS, (k + 1) * BS)
            out[0, k] = lax.dot_general(
                left[0, :, cols], right[:, cols], (((0,), (0,)), ((), ())),
                preferred_element_type=F32,
            ).astype(BF)
    gx[0] = e[:, 4 * tok:5 * tok, :].reshape(nsrc * tok, -1)


def weight_grads(tok, e, l2, r2, l1, r1, w_shape):
    vmem = pl.BlockSpec(memory_space=pltpu.VMEM)
    return pl.pallas_call(
        functools.partial(grads_kernel, tok),
        out_shape=(jax.ShapeDtypeStruct(l2.shape, BF),)
        + tuple(jax.ShapeDtypeStruct(w_shape, BF) for _ in range(4)),
        in_specs=[vmem] * 5,
        out_specs=(vmem,) * 5,
        compiler_params=pltpu.CompilerParams(vmem_limit_bytes=32 * 1024 * 1024),
        name="weight_grads",
    )(e, l2, r2, l1, r1)


def shards(
    grad_out, saved_input, saved_first, saved_pre, saved_second,
    right_one, left_one, right_two, left_two,
):
    me = lax.axis_index("pipe")
    nsec = lax.axis_size("pipe")
    nfeat = lax.axis_size("feat")
    ntok, width = grad_out.shape
    tok = ntok // nfeat

    at = lax.axis_index("feat")
    offsets = jnp.concatenate([(jnp.arange(NX) - at // NZ) % NX, (jnp.arange(NZ) - at % NZ) % NZ])

    both = jnp.concatenate(
        [saved_pre[0].reshape(nfeat, tok, width), grad_out.reshape(nfeat, tok, width)], axis=1
    )
    pieces, both = gathered(*pack(left_two, right_two, left_one, right_one), both)
    z = both[:, :tok].astype(F32)
    dy = both[:, tok:]
    cdf = 0.5 * (1.0 + lax.erf(z * 0.7071067811865476))
    slope = cdf + z * jnp.exp(-0.5 * z * z) * 0.3989422804014327
    zf = saved_pre.astype(F32)
    act = (zf * (0.5 * (1.0 + lax.erf(zf * 0.7071067811865476)))).astype(BF)

    e = blank((nfeat, 5 * tok, width))
    for turn in range(nsec):
        sec = nsec - 1 - turn
        where = jnp.concatenate([(me == sec).astype(jnp.int32).reshape(1), offsets.astype(jnp.int32)])
        if sec > 0:
            e, gx = section(where, dy, slope, pieces, e)
            dy = lax.ppermute(gx, "pipe", [(sec, sec - 1)])
        else:
            e = section(where, dy, slope, pieces, e, last=True)
    e = lax.all_to_all(e, "feat", split_axis=0, concat_axis=0, tiled=True)
    return weight_grads(tok, e, saved_second, act, saved_first, saved_input, right_one.shape)


def solution(mesh):
    rows = P("pipe", None, "feat")
    blocks = P("pipe", "feat", None, None)
    return jax.shard_map(
        shards,
        mesh=mesh,
        in_specs=(P(None, "feat"),) + (rows,) * 4 + (blocks,) * 4,
        out_specs=(rows,) + (blocks,) * 4,
        check_vma=False,
    )
```

```python
import functools

import jax
import jax.numpy as jnp
from jax import lax
from jax.experimental import pallas as pl
from jax.experimental.pallas import tpu as pltpu
from jax.sharding import PartitionSpec as P

BS = 128
BF = jnp.bfloat16
F32 = jnp.float32
NX, NZ = 4, 8
X_SLOTS = ((0, 0), (1, 0), (3, 0), (2, 0), (2, 1))
Z_SLOTS = ((0, 0), (1, 0), (7, 0), (2, 0), (6, 0), (3, 0), (5, 0), (4, 0))


def permuted(src, dst, tok):
    nb = src.shape[0] // tok
    low = lax.broadcasted_iota(jnp.int32, (nb, BS), 1) < nb
    for t in range(0, tok, 2):
        a = src[pl.ds(t, nb, stride=tok), :]
        b = src[pl.ds(t + 1, nb, stride=tok), :]
        y = jnp.concatenate([a, b], axis=0).T
        top, bot = y[:nb], y[nb:]
        dst[pl.ds(t, nb, stride=tok), :] = jnp.where(low, top, pltpu.roll(bot, nb, 1))
        dst[pl.ds(t + 1, nb, stride=tok), :] = jnp.where(low, pltpu.roll(top, nb, 1), bot)


def section_kernel(last, npieces, where, dy, slope, e_old, *rest):
    pieces, rest = rest[:npieces], rest[npieces:]
    if last:
        e_hbm, wa, wb, s1, s2, w_sems, e, sems = rest
    else:
        e, gx, wa, wb, s1, s2, w_sems = rest
    nsrc, tok, width = dy.shape

    def rows(blk):
        return pl.ds(blk * tok, tok)

    @pl.when(where[0] == 1)
    def _():
        gets = []
        for held, slots, parts, f, nblk in (
            (wa, X_SLOTS, pieces[:len(X_SLOTS)], 0, 2),
            (wa, X_SLOTS, pieces[:len(X_SLOTS)], 1, 2),
            (wb, Z_SLOTS, pieces[len(X_SLOTS):], 0, 4),
        ):
            blocks = pl.ds(2 * f, nblk)
            base = sum(map(len, gets))
            gets.append([
                pltpu.make_async_copy(
                    part.at[:, blocks],
                    held.at[slot, pl.ds(half * part.shape[0], part.shape[0]), blocks],
                    w_sems.at[base + i],
                )
                for i, (part, (slot, half)) in enumerate(zip(parts, slots))
            ])
        for group in gets:
            for get in group:
                get.start()
        if last:
            puts = [
                pltpu.make_async_copy(
                    e.at[:, pl.ds(f * tok, tok)], e_hbm.at[:, pl.ds(f * tok, tok)], sems.at[f]
                )
                for f in range(5)
            ]
        first = lax.broadcasted_iota(jnp.int32, (tok, width), 1) < BS
        zero = jnp.zeros((tok, width), BF)
        for s in range(nsrc):
            for k in range(2):
                s1[rows(2 * s + k), :] = dy[s, :, k * BS:(k + 1) * BS].astype(F32)
        for f in range(4):
            permuted(s1, s2, tok)
            for get in gets[f] if f < 3 else []:
                get.wait()
            for s in range(nsrc):
                v = jnp.concatenate([s2[rows(2 * s), :].astype(BF), s2[rows(2 * s + 1), :].astype(BF)], axis=1)
                e[s, f * tok:(f + 1) * tok, :] = v
                pair = jnp.concatenate([jnp.where(first, v, zero), jnp.where(first, zero, v)], axis=0)
                rx, rz = where[1 + s // NZ], where[1 + NX + s % NZ]
                if f < 2:
                    mat = wa[rx, rz, 2 * f:2 * f + 2]
                else:
                    mat = wb[rz, rx, 2 * f - 4:2 * f - 2]
                out = jnp.dot(pair, mat.reshape(width, BS), preferred_element_type=F32)
                if f == 1:
                    out = out * jnp.concatenate([slope[s, :, :BS], slope[s, :, BS:]], axis=0)
                if f < 3:
                    s1[pl.ds(2 * s * tok, 2 * tok), :] = out.astype(BF).astype(F32)
                else:
                    out = jnp.concatenate([out[:tok], out[tok:]], axis=1)
                    out = (out + dy[s].astype(F32)).astype(BF)
                    e[s, 4 * tok:5 * tok, :] = out
                    if not last:
                        gx[s] = out
            if last:
                puts[f].start()
        if last:
            puts[4].start()
            for put in puts:
                put.wait()

    if last:
        @pl.when(where[0] == 0)
        def _():
            put = pltpu.make_async_copy(e_old, e_hbm, sems.at[0])
            put.start()
            put.wait()


def in_vmem(v):
    return pltpu.with_memory_space_constraint(v, pltpu.VMEM)


def section(where, dy, slope, pieces, e, last=False):
    nsrc, tok, width = dy.shape
    smem = pl.BlockSpec(memory_space=pltpu.SMEM)
    vmem = pl.BlockSpec(memory_space=pltpu.VMEM)
    anywhere = pl.BlockSpec(memory_space=pl.ANY)
    work = [
        pltpu.VMEM((NX, NZ, 4, BS, BS), BF),
        pltpu.VMEM((NZ, NX, 4, BS, BS), BF),
        pltpu.VMEM((nsrc * 2 * tok, BS), F32),
        pltpu.VMEM((nsrc * 2 * tok, BS), F32),
        pltpu.SemaphoreType.DMA((2 * len(pieces),)),
    ]
    if last:
        out_shape = jax.ShapeDtypeStruct(e.shape, BF)
        out_specs, aliases = anywhere, {}
        work += [pltpu.VMEM(e.shape, BF), pltpu.SemaphoreType.DMA((5,))]
    else:
        out_shape = (pltpu.VMEM(e.shape, BF), pltpu.VMEM(dy.shape, BF))
        out_specs, aliases = (vmem, vmem), {3: 0}
    return pl.pallas_call(
        functools.partial(section_kernel, last, len(pieces)),
        out_shape=out_shape,
        in_specs=[smem, vmem, vmem, vmem] + [anywhere] * len(pieces),
        out_specs=out_specs,
        input_output_aliases=aliases,
        scratch_shapes=work,
        compiler_params=pltpu.CompilerParams(vmem_limit_bytes=20 * 1024 * 1024),
        name="section",
    )(
        where, in_vmem(dy), in_vmem(slope), in_vmem(e),
        *[pltpu.with_memory_space_constraint(p, pltpu.HBM) for p in pieces],
    )


def shift(v, dx, dz):
    route = [
        (x * NZ + z, (x + dx) % NX * NZ + (z + dz) % NZ) for x in range(NX) for z in range(NZ)
    ]
    return lax.ppermute(v, "feat", route)


def along_z(v):
    up, down = shift(v, 0, -1), shift(v, 0, 1)
    out = [v, up, down]
    for _ in range(2):
        up, down = shift(up, 0, -1), shift(down, 0, 1)
        out += [up, down]
    return out + [shift(up, 0, -1)]


def gathered(two, one, both):
    one = jnp.stack([one, shift(one, -1, 0), shift(one, 2, 0), shift(one, 1, 0)])
    both = lax.all_to_all(both, "feat", split_axis=0, concat_axis=0, tiled=True)
    own, u1, d1, u2, d2, u3, d3, u4 = along_z(two)
    one, _ = lax.optimization_barrier((one, u2))
    two = jnp.stack([own, u1, u2, u3, u4, d3, d2, d1])
    up, down = shift(one, 0, -1), shift(one, 0, 1)
    by_z = [one, up, down]
    x_up, x_down = shift(two, -1, 0), shift(two, 1, 0)
    up, down = shift(up, 0, -1), shift(down, 0, 1)
    by_z += [up, down]
    up, down, _, _ = lax.optimization_barrier((up, down, x_up, x_down))
    up, down = shift(up, 0, -1), shift(down, 0, 1)
    by_z += [up, down]
    by_z += [shift(up, 0, -1)]
    half = NZ // 2
    by_x = [two, x_up, x_down, shift(x_up[:half], -1, 0), shift(x_down[half:], 1, 0)]
    return by_x + by_z, both


def blank_kernel(e):
    e[0] = jnp.zeros(e.shape[1:], BF)


def blank(shape):
    return pl.pallas_call(
        blank_kernel,
        out_shape=pltpu.VMEM(shape, BF),
        out_specs=pl.BlockSpec(memory_space=pltpu.VMEM),
        name="blank",
    )()


def pack_kernel(l2, r2, l1, r1, two, one):
    for f, w in enumerate((l2, r2, l1, r1)):
        for k in range(2):
            (two, one)[f // 2][2 * (f % 2) + k] = w[0, k].astype(F32).T.astype(BF)


def pack(l2, r2, l1, r1):
    vmem = pl.BlockSpec(memory_space=pltpu.VMEM)
    return pl.pallas_call(
        pack_kernel,
        out_shape=(jax.ShapeDtypeStruct((4, BS, BS), BF),) * 2,
        in_specs=[vmem] * 4,
        out_specs=(vmem, vmem),
        name="pack",
    )(l2, r2, l1, r1)


def grads_kernel(tok, e, l2, r2, l1, r1, gx, g_r1, g_l1, g_r2, g_l2):
    nsrc = e.shape[0]
    for f, (left, out) in enumerate(((l2, g_l2), (r2, g_r2), (l1, g_l1), (r1, g_r1))):
        right = e[:, f * tok:(f + 1) * tok, :].reshape(nsrc * tok, -1)
        for k in range(2):
            cols = slice(k * BS, (k + 1) * BS)
            out[0, k] = lax.dot_general(
                left[0, :, cols], right[:, cols], (((0,), (0,)), ((), ())),
                preferred_element_type=F32,
            ).astype(BF)
    gx[0] = e[:, 4 * tok:5 * tok, :].reshape(nsrc * tok, -1)


def weight_grads(tok, e, l2, r2, l1, r1, w_shape):
    vmem = pl.BlockSpec(memory_space=pltpu.VMEM)
    return pl.pallas_call(
        functools.partial(grads_kernel, tok),
        out_shape=(jax.ShapeDtypeStruct(l2.shape, BF),)
        + tuple(jax.ShapeDtypeStruct(w_shape, BF) for _ in range(4)),
        in_specs=[vmem] * 5,
        out_specs=(vmem,) * 5,
        compiler_params=pltpu.CompilerParams(vmem_limit_bytes=32 * 1024 * 1024),
        name="weight_grads",
    )(e, l2, r2, l1, r1)


def shards(
    grad_out, saved_input, saved_first, saved_pre, saved_second,
    right_one, left_one, right_two, left_two,
):
    me = lax.axis_index("pipe")
    nsec = lax.axis_size("pipe")
    nfeat = lax.axis_size("feat")
    ntok, width = grad_out.shape
    tok = ntok // nfeat

    at = lax.axis_index("feat")
    offsets = jnp.concatenate([(jnp.arange(NX) - at // NZ) % NX, (jnp.arange(NZ) - at % NZ) % NZ])

    both = jnp.concatenate(
        [saved_pre[0].reshape(nfeat, tok, width), grad_out.reshape(nfeat, tok, width)], axis=1
    )
    pieces, both = gathered(*pack(left_two, right_two, left_one, right_one), both)
    z = both[:, :tok].astype(F32)
    dy = both[:, tok:]
    cdf = 0.5 * (1.0 + lax.erf(z * 0.7071067811865476))
    slope = cdf + z * jnp.exp(-0.5 * z * z) * 0.3989422804014327
    zf = saved_pre.astype(F32)
    act = (zf * (0.5 * (1.0 + lax.erf(zf * 0.7071067811865476)))).astype(BF)

    e = blank((nfeat, 5 * tok, width))
    for turn in range(nsec):
        sec = nsec - 1 - turn
        where = jnp.concatenate([(me == sec).astype(jnp.int32).reshape(1), offsets.astype(jnp.int32)])
        if sec > 0:
            e, gx = section(where, dy, slope, pieces, e)
            dy = lax.ppermute(gx, "pipe", [(sec, sec - 1)])
        else:
            e = section(where, dy, slope, pieces, e, last=True)
    e = lax.all_to_all(e, "feat", split_axis=0, concat_axis=0, tiled=True)
    return weight_grads(tok, e, saved_second, act, saved_first, saved_input, right_one.shape)


def solution(mesh):
    rows = P("pipe", None, "feat")
    blocks = P("pipe", "feat", None, None)
    return jax.shard_map(
        shards,
        mesh=mesh,
        in_specs=(P(None, "feat"),) + (rows,) * 4 + (blocks,) * 4,
        out_specs=(rows,) + (blocks,) * 4,
        check_vma=False,
    )
```

```python
import functools

import jax
import jax.numpy as jnp
from jax import lax
from jax.experimental import pallas as pl
from jax.experimental.pallas import tpu as pltpu
from jax.sharding import PartitionSpec as P

BS = 128
BF = jnp.bfloat16
F32 = jnp.float32
NX, NZ = 4, 8
X_SLOTS = ((0, 0), (1, 0), (3, 0), (2, 0), (2, 1))
Z_SLOTS = ((0, 0), (1, 0), (7, 0), (2, 0), (6, 0), (3, 0), (5, 0), (4, 0))


def permuted(src, dst, tok):
    nb = src.shape[0] // tok
    low = lax.broadcasted_iota(jnp.int32, (nb, BS), 1) < nb
    for t in range(0, tok, 2):
        a = src[pl.ds(t, nb, stride=tok), :]
        b = src[pl.ds(t + 1, nb, stride=tok), :]
        y = jnp.concatenate([a, b], axis=0).T
        top, bot = y[:nb], y[nb:]
        dst[pl.ds(t, nb, stride=tok), :] = jnp.where(low, top, pltpu.roll(bot, nb, 1))
        dst[pl.ds(t + 1, nb, stride=tok), :] = jnp.where(low, pltpu.roll(top, nb, 1), bot)


def section_kernel(last, npieces, where, dy, slope, e_old, *rest):
    pieces, rest = rest[:npieces], rest[npieces:]
    if last:
        e_hbm, wa, wb, s1, s2, w_sems, e, sems = rest
    else:
        e, gx, wa, wb, s1, s2, w_sems = rest
    nsrc, tok, width = dy.shape

    def rows(blk):
        return pl.ds(blk * tok, tok)

    @pl.when(where[0] == 1)
    def _():
        gets = []
        for held, slots, parts, f, nblk in (
            (wa, X_SLOTS, pieces[:len(X_SLOTS)], 0, 2),
            (wa, X_SLOTS, pieces[:len(X_SLOTS)], 1, 2),
            (wb, Z_SLOTS, pieces[len(X_SLOTS):], 0, 4),
        ):
            blocks = pl.ds(2 * f, nblk)
            base = sum(map(len, gets))
            gets.append([
                pltpu.make_async_copy(
                    part.at[:, blocks],
                    held.at[slot, pl.ds(half * part.shape[0], part.shape[0]), blocks],
                    w_sems.at[base + i],
                )
                for i, (part, (slot, half)) in enumerate(zip(parts, slots))
            ])
        for group in gets:
            for get in group:
                get.start()
        if last:
            puts = [
                pltpu.make_async_copy(
                    e.at[:, pl.ds(f * tok, tok)], e_hbm.at[:, pl.ds(f * tok, tok)], sems.at[f]
                )
                for f in range(5)
            ]
        first = lax.broadcasted_iota(jnp.int32, (tok, width), 1) < BS
        zero = jnp.zeros((tok, width), BF)
        for s in range(nsrc):
            for k in range(2):
                s1[rows(2 * s + k), :] = dy[s, :, k * BS:(k + 1) * BS].astype(F32)
        for f in range(4):
            permuted(s1, s2, tok)
            for get in gets[f] if f < 3 else []:
                get.wait()
            for s in range(nsrc):
                v = jnp.concatenate([s2[rows(2 * s), :].astype(BF), s2[rows(2 * s + 1), :].astype(BF)], axis=1)
                e[s, f * tok:(f + 1) * tok, :] = v
                pair = jnp.concatenate([jnp.where(first, v, zero), jnp.where(first, zero, v)], axis=0)
                rx, rz = where[1 + s // NZ], where[1 + NX + s % NZ]
                if f < 2:
                    mat = wa[rx, rz, 2 * f:2 * f + 2]
                else:
                    mat = wb[rz, rx, 2 * f - 4:2 * f - 2]
                out = jnp.dot(pair, mat.reshape(width, BS), preferred_element_type=F32)
                if f == 1:
                    out = out * jnp.concatenate([slope[s, :, :BS], slope[s, :, BS:]], axis=0)
                if f < 3:
                    s1[pl.ds(2 * s * tok, 2 * tok), :] = out.astype(BF).astype(F32)
                else:
                    out = jnp.concatenate([out[:tok], out[tok:]], axis=1)
                    out = (out + dy[s].astype(F32)).astype(BF)
                    e[s, 4 * tok:5 * tok, :] = out
                    if not last:
                        gx[s] = out
            if last:
                puts[f].start()
        if last:
            puts[4].start()
            for put in puts:
                put.wait()

    if last:
        @pl.when(where[0] == 0)
        def _():
            put = pltpu.make_async_copy(e_old, e_hbm, sems.at[0])
            put.start()
            put.wait()


def in_vmem(v):
    return pltpu.with_memory_space_constraint(v, pltpu.VMEM)


def section(where, dy, slope, pieces, e, last=False):
    nsrc, tok, width = dy.shape
    smem = pl.BlockSpec(memory_space=pltpu.SMEM)
    vmem = pl.BlockSpec(memory_space=pltpu.VMEM)
    anywhere = pl.BlockSpec(memory_space=pl.ANY)
    work = [
        pltpu.VMEM((NX, NZ, 4, BS, BS), BF),
        pltpu.VMEM((NZ, NX, 4, BS, BS), BF),
        pltpu.VMEM((nsrc * 2 * tok, BS), F32),
        pltpu.VMEM((nsrc * 2 * tok, BS), F32),
        pltpu.SemaphoreType.DMA((2 * len(pieces),)),
    ]
    if last:
        out_shape = jax.ShapeDtypeStruct(e.shape, BF)
        out_specs, aliases = anywhere, {}
        work += [pltpu.VMEM(e.shape, BF), pltpu.SemaphoreType.DMA((5,))]
    else:
        out_shape = (pltpu.VMEM(e.shape, BF), pltpu.VMEM(dy.shape, BF))
        out_specs, aliases = (vmem, vmem), {3: 0}
    return pl.pallas_call(
        functools.partial(section_kernel, last, len(pieces)),
        out_shape=out_shape,
        in_specs=[smem, vmem, vmem, vmem] + [anywhere] * len(pieces),
        out_specs=out_specs,
        input_output_aliases=aliases,
        scratch_shapes=work,
        compiler_params=pltpu.CompilerParams(vmem_limit_bytes=20 * 1024 * 1024),
        name="section",
    )(
        where, in_vmem(dy), in_vmem(slope), in_vmem(e),
        *[pltpu.with_memory_space_constraint(p, pltpu.HBM) for p in pieces],
    )


def shift(v, dx, dz):
    route = [
        (x * NZ + z, (x + dx) % NX * NZ + (z + dz) % NZ) for x in range(NX) for z in range(NZ)
    ]
    return lax.ppermute(v, "feat", route)


def along_z(v):
    up, down = shift(v, 0, -1), shift(v, 0, 1)
    out = [v, up, down]
    for _ in range(2):
        up, down = shift(up, 0, -1), shift(down, 0, 1)
        out += [up, down]
    return out + [shift(up, 0, -1)]


def gathered(two, one, both):
    one = jnp.stack([one, shift(one, -1, 0), shift(one, 2, 0), shift(one, 1, 0)])
    both = lax.all_to_all(both, "feat", split_axis=0, concat_axis=0, tiled=True)
    own, u1, d1, u2, d2, u3, d3, u4 = along_z(two)
    one, _ = lax.optimization_barrier((one, u3))
    two = jnp.stack([own, u1, u2, u3, u4, d3, d2, d1])
    up, down = shift(one, 0, -1), shift(one, 0, 1)
    by_z = [one, up, down]
    x_up, x_down = shift(two, -1, 0), shift(two, 1, 0)
    up, down = shift(up, 0, -1), shift(down, 0, 1)
    by_z += [up, down]
    up, down, _, _ = lax.optimization_barrier((up, down, x_up, x_down))
    up, down = shift(up, 0, -1), shift(down, 0, 1)
    by_z += [up, down]
    by_z += [shift(up, 0, -1)]
    half = NZ // 2
    by_x = [two, x_up, x_down, shift(x_up[:half], -1, 0), shift(x_down[half:], 1, 0)]
    return by_x + by_z, both


def blank_kernel(e):
    e[0] = jnp.zeros(e.shape[1:], BF)


def blank(shape):
    return pl.pallas_call(
        blank_kernel,
        out_shape=pltpu.VMEM(shape, BF),
        out_specs=pl.BlockSpec(memory_space=pltpu.VMEM),
        name="blank",
    )()


def pack_kernel(l2, r2, l1, r1, two, one):
    for f, w in enumerate((l2, r2, l1, r1)):
        for k in range(2):
            (two, one)[f // 2][2 * (f % 2) + k] = w[0, k].astype(F32).T.astype(BF)


def pack(l2, r2, l1, r1):
    vmem = pl.BlockSpec(memory_space=pltpu.VMEM)
    return pl.pallas_call(
        pack_kernel,
        out_shape=(jax.ShapeDtypeStruct((4, BS, BS), BF),) * 2,
        in_specs=[vmem] * 4,
        out_specs=(vmem, vmem),
        name="pack",
    )(l2, r2, l1, r1)


def grads_kernel(tok, e, l2, r2, l1, r1, gx, g_r1, g_l1, g_r2, g_l2):
    nsrc = e.shape[0]
    for f, (left, out) in enumerate(((l2, g_l2), (r2, g_r2), (l1, g_l1), (r1, g_r1))):
        right = e[:, f * tok:(f + 1) * tok, :].reshape(nsrc * tok, -1)
        for k in range(2):
            cols = slice(k * BS, (k + 1) * BS)
            out[0, k] = lax.dot_general(
                left[0, :, cols], right[:, cols], (((0,), (0,)), ((), ())),
                preferred_element_type=F32,
            ).astype(BF)
    gx[0] = e[:, 4 * tok:5 * tok, :].reshape(nsrc * tok, -1)


def weight_grads(tok, e, l2, r2, l1, r1, w_shape):
    vmem = pl.BlockSpec(memory_space=pltpu.VMEM)
    return pl.pallas_call(
        functools.partial(grads_kernel, tok),
        out_shape=(jax.ShapeDtypeStruct(l2.shape, BF),)
        + tuple(jax.ShapeDtypeStruct(w_shape, BF) for _ in range(4)),
        in_specs=[vmem] * 5,
        out_specs=(vmem,) * 5,
        compiler_params=pltpu.CompilerParams(vmem_limit_bytes=32 * 1024 * 1024),
        name="weight_grads",
    )(e, l2, r2, l1, r1)


def shards(
    grad_out, saved_input, saved_first, saved_pre, saved_second,
    right_one, left_one, right_two, left_two,
):
    me = lax.axis_index("pipe")
    nsec = lax.axis_size("pipe")
    nfeat = lax.axis_size("feat")
    ntok, width = grad_out.shape
    tok = ntok // nfeat

    at = lax.axis_index("feat")
    offsets = jnp.concatenate([(jnp.arange(NX) - at // NZ) % NX, (jnp.arange(NZ) - at % NZ) % NZ])

    both = jnp.concatenate(
        [saved_pre[0].reshape(nfeat, tok, width), grad_out.reshape(nfeat, tok, width)], axis=1
    )
    pieces, both = gathered(*pack(left_two, right_two, left_one, right_one), both)
    z = both[:, :tok].astype(F32)
    dy = both[:, tok:]
    cdf = 0.5 * (1.0 + lax.erf(z * 0.7071067811865476))
    slope = cdf + z * jnp.exp(-0.5 * z * z) * 0.3989422804014327
    zf = saved_pre.astype(F32)
    act = (zf * (0.5 * (1.0 + lax.erf(zf * 0.7071067811865476)))).astype(BF)

    e = blank((nfeat, 5 * tok, width))
    for turn in range(nsec):
        sec = nsec - 1 - turn
        where = jnp.concatenate([(me == sec).astype(jnp.int32).reshape(1), offsets.astype(jnp.int32)])
        if sec > 0:
            e, gx = section(where, dy, slope, pieces, e)
            dy = lax.ppermute(gx, "pipe", [(sec, sec - 1)])
        else:
            e = section(where, dy, slope, pieces, e, last=True)
    e = lax.all_to_all(e, "feat", split_axis=0, concat_axis=0, tiled=True)
    return weight_grads(tok, e, saved_second, act, saved_first, saved_input, right_one.shape)


def solution(mesh):
    rows = P("pipe", None, "feat")
    blocks = P("pipe", "feat", None, None)
    return jax.shard_map(
        shards,
        mesh=mesh,
        in_specs=(P(None, "feat"),) + (rows,) * 4 + (blocks,) * 4,
        out_specs=(rows,) + (blocks,) * 4,
        check_vma=False,
    )
```

```python
import functools

import jax
import jax.numpy as jnp
from jax import lax
from jax.experimental import pallas as pl
from jax.experimental.pallas import tpu as pltpu
from jax.sharding import PartitionSpec as P

BS = 128
BF = jnp.bfloat16
F32 = jnp.float32
NX, NZ = 4, 8
X_SLOTS = ((0, 0), (1, 0), (3, 0), (2, 0), (2, 1))
Z_SLOTS = ((0, 0), (1, 0), (7, 0), (2, 0), (6, 0), (3, 0), (5, 0), (4, 0))


def permuted(src, dst, tok):
    nb = src.shape[0] // tok
    low = lax.broadcasted_iota(jnp.int32, (nb, BS), 1) < nb
    for t in range(0, tok, 2):
        a = src[pl.ds(t, nb, stride=tok), :]
        b = src[pl.ds(t + 1, nb, stride=tok), :]
        y = jnp.concatenate([a, b], axis=0).T
        top, bot = y[:nb], y[nb:]
        dst[pl.ds(t, nb, stride=tok), :] = jnp.where(low, top, pltpu.roll(bot, nb, 1))
        dst[pl.ds(t + 1, nb, stride=tok), :] = jnp.where(low, pltpu.roll(top, nb, 1), bot)


def section_kernel(last, npieces, where, dy, slope, e_old, *rest):
    pieces, rest = rest[:npieces], rest[npieces:]
    if last:
        e_hbm, wa, wb, s1, s2, w_sems, e, sems = rest
    else:
        e, gx, wa, wb, s1, s2, w_sems = rest
    nsrc, tok, width = dy.shape

    def rows(blk):
        return pl.ds(blk * tok, tok)

    @pl.when(where[0] == 1)
    def _():
        gets = []
        for held, slots, parts, f, nblk in (
            (wa, X_SLOTS, pieces[:len(X_SLOTS)], 0, 2),
            (wa, X_SLOTS, pieces[:len(X_SLOTS)], 1, 2),
            (wb, Z_SLOTS, pieces[len(X_SLOTS):], 0, 4),
        ):
            blocks = pl.ds(2 * f, nblk)
            base = sum(map(len, gets))
            gets.append([
                pltpu.make_async_copy(
                    part.at[:, blocks],
                    held.at[slot, pl.ds(half * part.shape[0], part.shape[0]), blocks],
                    w_sems.at[base + i],
                )
                for i, (part, (slot, half)) in enumerate(zip(parts, slots))
            ])
        for group in gets:
            for get in group:
                get.start()
        if last:
            puts = [
                pltpu.make_async_copy(
                    e.at[:, pl.ds(f * tok, tok)], e_hbm.at[:, pl.ds(f * tok, tok)], sems.at[f]
                )
                for f in range(5)
            ]
        first = lax.broadcasted_iota(jnp.int32, (tok, width), 1) < BS
        zero = jnp.zeros((tok, width), BF)
        for s in range(nsrc):
            for k in range(2):
                s1[rows(2 * s + k), :] = dy[s, :, k * BS:(k + 1) * BS].astype(F32)
        for f in range(4):
            permuted(s1, s2, tok)
            for get in gets[f] if f < 3 else []:
                get.wait()
            for s in range(nsrc):
                v = jnp.concatenate([s2[rows(2 * s), :].astype(BF), s2[rows(2 * s + 1), :].astype(BF)], axis=1)
                e[s, f * tok:(f + 1) * tok, :] = v
                pair = jnp.concatenate([jnp.where(first, v, zero), jnp.where(first, zero, v)], axis=0)
                rx, rz = where[1 + s // NZ], where[1 + NX + s % NZ]
                if f < 2:
                    mat = wa[rx, rz, 2 * f:2 * f + 2]
                else:
                    mat = wb[rz, rx, 2 * f - 4:2 * f - 2]
                out = jnp.dot(pair, mat.reshape(width, BS), preferred_element_type=F32)
                if f == 1:
                    out = out * jnp.concatenate([slope[s, :, :BS], slope[s, :, BS:]], axis=0)
                if f < 3:
                    s1[pl.ds(2 * s * tok, 2 * tok), :] = out.astype(BF).astype(F32)
                else:
                    out = jnp.concatenate([out[:tok], out[tok:]], axis=1)
                    out = (out + dy[s].astype(F32)).astype(BF)
                    e[s, 4 * tok:5 * tok, :] = out
                    if not last:
                        gx[s] = out
            if last:
                puts[f].start()
        if last:
            puts[4].start()
            for put in puts:
                put.wait()

    if last:
        @pl.when(where[0] == 0)
        def _():
            put = pltpu.make_async_copy(e_old, e_hbm, sems.at[0])
            put.start()
            put.wait()


def in_vmem(v):
    return pltpu.with_memory_space_constraint(v, pltpu.VMEM)


def section(where, dy, slope, pieces, e, last=False):
    nsrc, tok, width = dy.shape
    smem = pl.BlockSpec(memory_space=pltpu.SMEM)
    vmem = pl.BlockSpec(memory_space=pltpu.VMEM)
    anywhere = pl.BlockSpec(memory_space=pl.ANY)
    work = [
        pltpu.VMEM((NX, NZ, 4, BS, BS), BF),
        pltpu.VMEM((NZ, NX, 4, BS, BS), BF),
        pltpu.VMEM((nsrc * 2 * tok, BS), F32),
        pltpu.VMEM((nsrc * 2 * tok, BS), F32),
        pltpu.SemaphoreType.DMA((2 * len(pieces),)),
    ]
    if last:
        out_shape = jax.ShapeDtypeStruct(e.shape, BF)
        out_specs, aliases = anywhere, {}
        work += [pltpu.VMEM(e.shape, BF), pltpu.SemaphoreType.DMA((5,))]
    else:
        out_shape = (pltpu.VMEM(e.shape, BF), pltpu.VMEM(dy.shape, BF))
        out_specs, aliases = (vmem, vmem), {3: 0}
    return pl.pallas_call(
        functools.partial(section_kernel, last, len(pieces)),
        out_shape=out_shape,
        in_specs=[smem, vmem, vmem, vmem] + [anywhere] * len(pieces),
        out_specs=out_specs,
        input_output_aliases=aliases,
        scratch_shapes=work,
        compiler_params=pltpu.CompilerParams(vmem_limit_bytes=20 * 1024 * 1024),
        name="section",
    )(
        where, in_vmem(dy), in_vmem(slope), in_vmem(e),
        *[pltpu.with_memory_space_constraint(p, pltpu.HBM) for p in pieces],
    )


def shift(v, dx, dz):
    route = [
        (x * NZ + z, (x + dx) % NX * NZ + (z + dz) % NZ) for x in range(NX) for z in range(NZ)
    ]
    return lax.ppermute(v, "feat", route)


def along_z(v):
    up, down = shift(v, 0, -1), shift(v, 0, 1)
    out = [v, up, down]
    for _ in range(2):
        up, down = shift(up, 0, -1), shift(down, 0, 1)
        out += [up, down]
    return out + [shift(up, 0, -1)]


def gathered(two, one, both):
    one = jnp.stack([one, shift(one, -1, 0), shift(one, 2, 0), shift(one, 1, 0)])
    both = lax.all_to_all(both, "feat", split_axis=0, concat_axis=0, tiled=True)
    own, u1, d1, u2, d2, u3, d3, u4 = along_z(two)
    one, _ = lax.optimization_barrier((one, u4))
    two = jnp.stack([own, u1, u2, u3, u4, d3, d2, d1])
    up, down = shift(one, 0, -1), shift(one, 0, 1)
    by_z = [one, up, down]
    x_up, x_down = shift(two, -1, 0), shift(two, 1, 0)
    up, down = shift(up, 0, -1), shift(down, 0, 1)
    by_z += [up, down]
    up, down, _, _ = lax.optimization_barrier((up, down, x_up, x_down))
    up, down = shift(up, 0, -1), shift(down, 0, 1)
    by_z += [up, down]
    by_z += [shift(up, 0, -1)]
    half = NZ // 2
    by_x = [two, x_up, x_down, shift(x_up[:half], -1, 0), shift(x_down[half:], 1, 0)]
    return by_x + by_z, both


def blank_kernel(e):
    e[0] = jnp.zeros(e.shape[1:], BF)


def blank(shape):
    return pl.pallas_call(
        blank_kernel,
        out_shape=pltpu.VMEM(shape, BF),
        out_specs=pl.BlockSpec(memory_space=pltpu.VMEM),
        name="blank",
    )()


def pack_kernel(l2, r2, l1, r1, two, one):
    for f, w in enumerate((l2, r2, l1, r1)):
        for k in range(2):
            (two, one)[f // 2][2 * (f % 2) + k] = w[0, k].astype(F32).T.astype(BF)


def pack(l2, r2, l1, r1):
    vmem = pl.BlockSpec(memory_space=pltpu.VMEM)
    return pl.pallas_call(
        pack_kernel,
        out_shape=(jax.ShapeDtypeStruct((4, BS, BS), BF),) * 2,
        in_specs=[vmem] * 4,
        out_specs=(vmem, vmem),
        name="pack",
    )(l2, r2, l1, r1)


def grads_kernel(tok, e, l2, r2, l1, r1, gx, g_r1, g_l1, g_r2, g_l2):
    nsrc = e.shape[0]
    for f, (left, out) in enumerate(((l2, g_l2), (r2, g_r2), (l1, g_l1), (r1, g_r1))):
        right = e[:, f * tok:(f + 1) * tok, :].reshape(nsrc * tok, -1)
        for k in range(2):
            cols = slice(k * BS, (k + 1) * BS)
            out[0, k] = lax.dot_general(
                left[0, :, cols], right[:, cols], (((0,), (0,)), ((), ())),
                preferred_element_type=F32,
            ).astype(BF)
    gx[0] = e[:, 4 * tok:5 * tok, :].reshape(nsrc * tok, -1)


def weight_grads(tok, e, l2, r2, l1, r1, w_shape):
    vmem = pl.BlockSpec(memory_space=pltpu.VMEM)
    return pl.pallas_call(
        functools.partial(grads_kernel, tok),
        out_shape=(jax.ShapeDtypeStruct(l2.shape, BF),)
        + tuple(jax.ShapeDtypeStruct(w_shape, BF) for _ in range(4)),
        in_specs=[vmem] * 5,
        out_specs=(vmem,) * 5,
        compiler_params=pltpu.CompilerParams(vmem_limit_bytes=32 * 1024 * 1024),
        name="weight_grads",
    )(e, l2, r2, l1, r1)


def shards(
    grad_out, saved_input, saved_first, saved_pre, saved_second,
    right_one, left_one, right_two, left_two,
):
    me = lax.axis_index("pipe")
    nsec = lax.axis_size("pipe")
    nfeat = lax.axis_size("feat")
    ntok, width = grad_out.shape
    tok = ntok // nfeat

    at = lax.axis_index("feat")
    offsets = jnp.concatenate([(jnp.arange(NX) - at // NZ) % NX, (jnp.arange(NZ) - at % NZ) % NZ])

    both = jnp.concatenate(
        [saved_pre[0].reshape(nfeat, tok, width), grad_out.reshape(nfeat, tok, width)], axis=1
    )
    pieces, both = gathered(*pack(left_two, right_two, left_one, right_one), both)
    z = both[:, :tok].astype(F32)
    dy = both[:, tok:]
    cdf = 0.5 * (1.0 + lax.erf(z * 0.7071067811865476))
    slope = cdf + z * jnp.exp(-0.5 * z * z) * 0.3989422804014327
    zf = saved_pre.astype(F32)
    act = (zf * (0.5 * (1.0 + lax.erf(zf * 0.7071067811865476)))).astype(BF)

    e = blank((nfeat, 5 * tok, width))
    for turn in range(nsec):
        sec = nsec - 1 - turn
        where = jnp.concatenate([(me == sec).astype(jnp.int32).reshape(1), offsets.astype(jnp.int32)])
        if sec > 0:
            e, gx = section(where, dy, slope, pieces, e)
            dy = lax.ppermute(gx, "pipe", [(sec, sec - 1)])
        else:
            e = section(where, dy, slope, pieces, e, last=True)
    e = lax.all_to_all(e, "feat", split_axis=0, concat_axis=0, tiled=True)
    return weight_grads(tok, e, saved_second, act, saved_first, saved_input, right_one.shape)


def solution(mesh):
    rows = P("pipe", None, "feat")
    blocks = P("pipe", "feat", None, None)
    return jax.shard_map(
        shards,
        mesh=mesh,
        in_specs=(P(None, "feat"),) + (rows,) * 4 + (blocks,) * 4,
        out_specs=(rows,) + (blocks,) * 4,
        check_vma=False,
    )
```
